32 devices in a mesh: grp: 2 (over x), seq: 8 (over z, y), row: 2 (over core).
Axes of the slice: x: 2, y: 2, z: 4, core: 2. Of those that a mesh axis runs over, the one named last changes fastest.
Arguments:
- left_act: bfloat16 [128, 256, 32], P(('grp', 'seq'), 'row'), parts along dimension 0, may hold values from -6 to 6
- right_act: bfloat16 [128, 384, 32], P(('grp', 'seq')), parts along dimension 0, may hold values from -6 to 6
- pair_grad: bfloat16 [512, 384, 128], P(('grp', 'row'), 'seq'), parts along dimension 0, may hold values from -24 to 24
- out_weight: bfloat16 [1024, 128], replicated, may hold values from -0.1875 to 0.1875
- seq_mask: int32 [128], P(('grp', 'seq')), parts along dimension 0, may hold values from 0 to 1, as said below
Outputs:
- grad_left: bfloat16 [128, 256, 32], P(('grp', 'seq'), 'row'), parts along dimension 0
- grad_right: bfloat16 [128, 384, 32], P(('grp', 'seq'), 'row'), parts along dimension 0
- grad_weight: float32 [2048, 128], P('grp'), parts along dimension 0
The draws below stay inside these ranges and needn't reach their ends.
There are 2 independent parts, one for each index of `grp`. The reference program is written for one: setup_inputs(seed, part) draws one part's arguments, and reference() takes and returns one part's arrays. A program takes and returns all parts, laid end to end along the dimension named above; an argument that names none is the same for every part. Nothing has to cross between parts.
Inputs may be any that keep to these rules, and one draw needn't show every extreme that they name: `seq_mask`: entry 0 (the query sequence) is 1.
All inputs are finite; a program needn't handle non-finite values.
Results may differ from the reference program's by a relative error of at most 0.001.
Values may be sent and summed in bfloat16 or wider, within the bound.
A program may use at most 128 MiB of HBM per device.

```python
import jax
import jax.numpy as jnp
from jax import lax

C = 32
K = 128
R = 384
S_DEV = 8
S = 64
RI = 256


def draw_seq_mask(key, part):
    key = jax.random.fold_in(key, 7)
    drawn = jax.random.randint(key, (S,), 0, 1000)
    limit = 900 - 600 * jnp.arange(S, dtype=jnp.int32) // S
    valid = (drawn < limit).astype(jnp.int32)
    return valid.at[0].set(1)


def level_of(rng, dims, cuts, smallest, top_value):
    level = 1.0
    for dim, shards_of in cuts:
        draws = jax.random.uniform(jax.random.fold_in(jax.random.fold_in(rng, 6), dim), (shards_of,), jnp.float32, smallest / len(cuts), top_value / len(cuts))
        level = level * jnp.repeat(jnp.exp(draws), dims[dim] // shards_of).reshape((-1,) + (1,) * (len(dims) - 1 - dim))
    return level


def scatter_about(key, dims, width, most, split=(), kind=jnp.bfloat16):
    level = level_of(key, dims, split, -0.22, 0.18) if split else 1.0
    values = jax.random.normal(key, dims, jnp.float32) * width * level
    return jnp.minimum(jnp.maximum(values, -most), most).astype(kind)


def setup_inputs(seed: int = 0, part: int = 0) -> dict:
    arg_keys = jax.random.split(jax.random.key(seed), 6)
    own_keys = jax.random.split(jax.random.fold_in(arg_keys[5], part), 6)
    left_act = scatter_about(own_keys[0], (S, RI, C), 1.0, 6.0, ((0, 8), (1, 2)))
    right_act = scatter_about(own_keys[1], (S, R, C), 1.0, 6.0, ((0, 8),))
    pair_grad = scatter_about(own_keys[2], (RI, R, K), 4.0, 24.0, ((0, 2), (1, 8)))
    out_weight = scatter_about(arg_keys[3], (C * C, K), (C * C) ** -0.5, 0.1875)
    seq_mask = draw_seq_mask(jax.random.fold_in(jax.random.fold_in(arg_keys[5], part), 71), part)
    return dict(left_act=left_act, right_act=right_act, pair_grad=pair_grad, out_weight=out_weight, seq_mask=seq_mask)


def reference(left_act, right_act, pair_grad, out_weight, seq_mask):
    hi = lax.Precision.HIGHEST
    mask_float = seq_mask.astype(jnp.float32)
    count = jnp.sum(mask_float)
    mask_half = mask_float.astype(jnp.bfloat16)[:, None, None]
    masked_left = left_act * mask_half
    masked_right = right_act * mask_half
    weight_cube = out_weight.reshape(C, C, K).astype(jnp.float32)
    pair_float = pair_grad.astype(jnp.float32)
    blocks = S // S_DEV
    left_blocks = masked_left.astype(jnp.float32).reshape(blocks, S_DEV, RI, C)
    right_blocks = masked_right.astype(jnp.float32).reshape(blocks, S_DEV, R, C)

    def one_block(carry, pieces):
        left_piece, right_piece = pieces
        partial_value = jnp.einsum("sjb,ijk->sibk", right_piece, pair_float, precision=hi)
        left_grad = jnp.einsum("sibk,abk->sia", partial_value, weight_cube, precision=hi)
        projected = jnp.einsum("sia,abk->sibk", left_piece, weight_cube, precision=hi)
        right_grad = jnp.einsum("sibk,ijk->sjb", projected, pair_float, precision=hi)
        carry = carry + jnp.einsum("sia,sibk->abk", left_piece, partial_value, precision=hi)
        return carry, (left_grad, right_grad)

    start = jnp.zeros((C, C, K), jnp.float32)
    total, (left_all, right_all) = lax.scan(one_block, start, (left_blocks, right_blocks))
    scale = (mask_float / count)[:, None, None]
    grad_left = (left_all.reshape(S, RI, C) * scale).astype(jnp.bfloat16)
    grad_right = (right_all.reshape(S, R, C) * scale).astype(jnp.bfloat16)
    grad_weight = (total / count).reshape(C * C, K)
    return grad_left, grad_right, grad_weight
```

```python
import functools

import jax
import jax.numpy as jnp
from jax import lax
from jax.experimental import pallas as pl
from jax.experimental.pallas import tpu as pltpu
from jax.sharding import PartitionSpec as P

NT = (((1,), (1,)), ((), ()))
NN = (((1,), (0,)), ((), ()))


def block_cols(cols):
    return max(n for n in (2, 4, 6, 8) if cols % n == 0)


def dot(lhs, rhs, dims):
    return lax.dot_general(lhs, rhs, dims, preferred_element_type=jnp.float32)


def split(value):
    high = value.astype(jnp.bfloat16)
    low = (value - high.astype(jnp.float32)).astype(jnp.bfloat16)
    return high, low


def kernel(chans, p_ref, w_ref, l_ref, r_ref, rt_ref, gl_ref, gr_ref, gw_ref, qh, ql, oh, ol):
    rows = p_ref.shape[1]
    pairs = p_ref.shape[0] // 2

    @pl.when(pl.program_id(0) == 0)
    def _():
        gl_ref[...] = jnp.zeros_like(gl_ref)
        gw_ref[...] = jnp.zeros_like(gw_ref)

    for jp in range(pairs):
        block = p_ref[2 * jp : 2 * jp + 2].reshape(2 * rows, -1)
        for ac in range(0, chans, 4):
            q = dot(w_ref[ac * chans : (ac + 4) * chans, :], block, NT)
            high, low = split(q)
            for a in range(4):
                for jj in range(2):
                    j = 2 * jp + jj
                    to = (slice(j * chans, (j + 1) * chans), slice((ac + a) * rows, (ac + a + 1) * rows))
                    at = (slice(a * chans, (a + 1) * chans), slice(jj * rows, (jj + 1) * rows))
                    qh[to] = high[at]
                    ql[to] = low[at]

    gr_ref[...] = dot(qh[...], l_ref[...], NT) + dot(ql[...], l_ref[...], NT)
    right = r_ref[0]
    for ac in range(0, chans, 2):
        at = slice(ac * rows, (ac + 2) * rows)
        gl_ref[:, at] += dot(right, qh[:, at], NN) + dot(right, ql[:, at], NN)

    right_t = rt_ref[...]
    for ac in range(0, chans, 2):
        at = slice(ac * rows, (ac + 2) * rows)
        o = dot(right_t, l_ref[:, at], NN)
        oh[:, at], ol[:, at] = split(o)

    for ac in range(0, chans, 8):
        total = gw_ref[ac * chans : (ac + 8) * chans, :]
        for jp in range(pairs):
            block = p_ref[2 * jp : 2 * jp + 2].reshape(2 * rows, -1)
            for src in (oh, ol):
                lhs = jnp.concatenate(
                    [
                        jnp.concatenate(
                            [
                                src[j * chans : (j + 1) * chans, a * rows : (a + 1) * rows]
                                for j in (2 * jp, 2 * jp + 1)
                            ],
                            axis=1,
                        )
                        for a in range(ac, ac + 8)
                    ],
                    axis=0,
                )
                total += dot(lhs, block, NN)
        gw_ref[ac * chans : (ac + 8) * chans, :] = total


def local_grads(pair_t, weight, left, right_b, right_t, chans):
    cols, rows, width = pair_t.shape
    seqs = left.shape[0]
    step_cols = block_cols(cols)
    steps = cols // step_cols
    jb = step_cols * chans
    flops = 2 * cols * rows * chans * chans * (width * 3 + seqs * 5)
    return pl.pallas_call(
        functools.partial(kernel, chans),
        grid=(steps,),
        in_specs=[
            pl.BlockSpec((step_cols, rows, width), lambda j: (j, 0, 0)),
            pl.BlockSpec((chans * chans, width), lambda j: (0, 0)),
            pl.BlockSpec((seqs, chans * rows), lambda j: (0, 0)),
            pl.BlockSpec((1, seqs, jb), lambda j: (j, 0, 0)),
            pl.BlockSpec((jb, seqs), lambda j: (j, 0)),
        ],
        out_specs=[
            pl.BlockSpec((seqs, chans * rows), lambda j: (0, 0)),
            pl.BlockSpec((jb, seqs), lambda j: (j, 0)),
            pl.BlockSpec((chans * chans, width), lambda j: (0, 0)),
        ],
        out_shape=[
            jax.ShapeDtypeStruct((seqs, chans * rows), jnp.float32),
            jax.ShapeDtypeStruct((cols * chans, seqs), jnp.float32),
            jax.ShapeDtypeStruct((chans * chans, width), jnp.float32),
        ],
        scratch_shapes=[pltpu.VMEM((jb, chans * rows), jnp.bfloat16)] * 4,
        compiler_params=pltpu.CompilerParams(vmem_limit_bytes=50 * 2**20),
        cost_estimate=pl.CostEstimate(flops=flops, bytes_accessed=6 * 2**20, transcendentals=0),
        name="local_grads",
    )(pair_t, weight, left, right_b, right_t)


def body(left_act, right_act, pair_grad, out_weight, seq_mask):
    seq_rows, pair_rows, chans = left_act.shape
    shards = lax.axis_size("seq")
    cols = right_act.shape[1]
    own = cols // shards
    mask_float = seq_mask.astype(jnp.float32)
    mask_half = mask_float.astype(jnp.bfloat16)[:, None, None]
    masked_left = (left_act * mask_half).transpose(0, 2, 1).reshape(seq_rows, chans * pair_rows)
    masked_right = (right_act * mask_half).reshape(seq_rows, cols * chans)
    pair_t = pair_grad.transpose(1, 0, 2)
    left = lax.all_gather(masked_left, "seq", axis=0, tiled=True)
    right = lax.all_to_all(masked_right, "seq", split_axis=1, concat_axis=0, tiled=True)
    seqs = left.shape[0]
    right_b = right.reshape(seqs, own // block_cols(own), -1).transpose(1, 0, 2)
    gl, gr, gw = local_grads(pair_t, out_weight, left, right_b, right.T, chans)
    count_total = lax.psum(jnp.sum(mask_float), "seq")
    weight_total = lax.psum(gw, ("seq", "row"))
    left_grad = lax.psum_scatter(gl, "seq", scatter_dimension=0, tiled=True)
    scale = mask_float / count_total
    left_grad = left_grad * scale[:, None]
    grad_left = left_grad.reshape(seq_rows, chans, pair_rows).transpose(0, 2, 1).astype(jnp.bfloat16)
    right_sum = lax.psum(gr, "row")
    right_all = lax.all_to_all(right_sum.T, "seq", split_axis=0, concat_axis=1, tiled=True)
    half = cols * chans // lax.axis_size("row")
    mine = lax.dynamic_slice_in_dim(right_all, lax.axis_index("row") * half, half, axis=1)
    grad_right = (mine * scale[:, None]).reshape(seq_rows, -1, chans).astype(jnp.bfloat16)
    return (grad_left, grad_right, weight_total / count_total)


def solution(mesh):
    placed = (
        P(("grp", "seq"), "row", None),
        P(("grp", "seq"), None, None),
        P(("grp", "row"), "seq", None),
        P(),
        P(("grp", "seq")),
    )
    return jax.shard_map(
        body,
        mesh=mesh,
        in_specs=placed,
        out_specs=(P(("grp", "seq"), "row", None), P(("grp", "seq"), "row", None), P("grp", None)),
        check_vma=False,
    )
```

```python
import functools

import jax
import jax.numpy as jnp
from jax import lax
from jax.experimental import pallas as pl
from jax.experimental.pallas import tpu as pltpu
from jax.sharding import PartitionSpec as P

NT = (((1,), (1,)), ((), ()))
NN = (((1,), (0,)), ((), ()))
MESH = pl.DeviceIdType.MESH
GL_LANES = 1024
LANE = 128


def block_cols(cols):
    return max(n for n in (2, 4, 6, 8) if cols % n == 0)


def dot(lhs, rhs, dims):
    return lax.dot_general(lhs, rhs, dims, preferred_element_type=jnp.float32)


def split(value):
    high = value.astype(jnp.bfloat16)
    low = (value - high.astype(jnp.float32)).astype(jnp.bfloat16)
    return high, low


def kernel(
    shards, chans, p_ref, w_ref, l_in, r_in, gl_out, gr_out, gw_out,
    qh, ql, oh, ol, l_all, r_all, left, right, right_t,
    part, gly, gls, glz, gr_t, gr_r, gr_b, gr_in,
    gw_acc, gw_r, gw_s1, gw_y, gw_s2, gw_z, gw_f,
    r_sem, lz_sem, ly_sem, gly_sem, glz_sem, grr_sem, gr_sem, gws_sem, gwz_sem, gwg_sem,
):
    cols, rows, width = p_ref.shape
    nz = shards // 2
    chunks = part.shape[0]
    seq_rows = l_in.shape[0]
    seqs = shards * seq_rows
    step_cols = block_cols(cols)
    steps = cols // step_cols
    jb = step_cols * chans
    own_cols = cols * chans
    me = lax.axis_index("seq")
    row = lax.axis_index("row")
    y, z = lax.rem(me, 2), lax.div(me, 2)
    ypeer, zs = z * 2 + 1 - y, [lax.rem(z + d, nz) for d in range(nz)]
    sent = []

    def send(src, dst, sems, at, where, recv_at=None):
        copy = pltpu.make_async_remote_copy(
            src_ref=src, dst_ref=dst, send_sem=sems.at[(0,) + at],
            recv_sem=sems.at[(1,) + (at if recv_at is None else recv_at)],
            device_id=where, device_id_type=MESH,
        )
        copy.start()
        return copy

    def arrive(dst, sems, at):
        pltpu.make_async_remote_copy(
            src_ref=dst, dst_ref=dst, send_sem=sems.at[(0,) + at], recv_sem=sems.at[(1,) + at],
            device_id={"seq": ypeer}, device_id_type=MESH,
        ).wait_recv()

    barrier = pltpu.get_barrier_semaphore()
    for o in range(1, shards):
        pl.semaphore_signal(barrier, inc=1, device_id={"seq": lax.rem(me + o, shards)}, device_id_type=MESH)
    pl.semaphore_signal(barrier, inc=1, device_id={"row": 1 - row}, device_id_type=MESH)
    pl.semaphore_wait(barrier, shards)

    for o in range(1, shards):
        e = lax.rem(me + o, shards)
        sent.append(send(r_in.at[e], r_all.at[me], r_sem, (o,), {"seq": e}))
    for d in range(1, nz):
        sent.append(send(l_in, l_all.at[me], lz_sem, (d,), {"seq": zs[d] * 2 + y}))
    sent.append(send(l_in, l_all.at[me], ly_sem, (0,), {"seq": ypeer}))
    l_all[me] = l_in[...]
    r_all[me] = r_in[me]

    def project(jp, carry):
        block = p_ref[pl.ds(jp * 2, 2)].reshape(2 * rows, width)
        for ac in range(0, chans, 4):
            q = dot(w_ref[ac * chans : (ac + 4) * chans, :], block, NT)
            high, low = split(q)
            for a in range(4):
                for jj in range(2):
                    base = pl.multiple_of((jp * 2 + jj) * chans, chans)
                    to = (pl.ds(base, chans), slice((ac + a) * rows, (ac + a + 1) * rows))
                    at = (slice(a * chans, (a + 1) * chans), slice(jj * rows, (jj + 1) * rows))
                    qh[to] = high[at]
                    ql[to] = low[at]
        return carry

    pairs = cols // 2
    lax.fori_loop(0, pairs // 2, project, 0)
    for d in range(1, nz):
        src = lax.rem(z + nz - d, nz) * 2 + y
        arrive(l_all.at[src], lz_sem, (d,))
        sent.append(send(l_all.at[src], l_all.at[src], ly_sem, (d,), {"seq": ypeer}))
    lax.fori_loop(pairs // 2, pairs, project, 0)

    for o in range(1, shards):
        arrive(r_all.at[lax.rem(me + shards - o, shards)], r_sem, (o,))
    rfull = r_all[...].astype(jnp.float32).reshape(seqs, LANE + own_cols)
    mask_all = rfull[:, :LANE]
    count = jnp.sum(mask_all, axis=0, keepdims=True)
    scale_all = mask_all / count
    scale_mine = r_in[me].astype(jnp.float32)[:, :LANE] / count
    right[...] = rfull[:, LANE:].astype(jnp.bfloat16)
    right_t[...] = rfull[:, LANE:].T.astype(jnp.bfloat16)

    for c in range(chunks):
        for t in range(0, GL_LANES, 256):
            at = slice(c * GL_LANES + t, c * GL_LANES + t + 256)
            g = dot(right[...], qh[:, at], NN) + dot(right[...], ql[:, at], NN)
            g = g.reshape(nz, 2, seq_rows, 256)
            for half in range(2):
                part[c, half, :, :, t : t + 256] = g[:, half]
        sent.append(send(part.at[c, 1 - y], gly.at[c], gly_sem, (c,), {"seq": ypeer}))

    for d in range(nz):
        src = lax.rem(z + nz - d, nz) * 2 + 1 - y
        arrive(l_all.at[src], ly_sem, (d,))
    left[...] = l_all[...].astype(jnp.float32).reshape(seqs, -1).astype(jnp.bfloat16)

    def gl_second(c):
        arrive(gly.at[c], gly_sem, (c,))
        gls[c] = part[c, y] + gly[c]
        for d in range(1, nz):
            sent.append(send(gls.at[c, zs[d]], glz.at[c, z], glz_sem, (c, d), {"seq": zs[d] * 2 + y}))

    def gl_last(c):
        total = gls[c, z]
        for d in range(1, nz):
            src = lax.rem(z + nz - d, nz)
            arrive(glz.at[c, src], glz_sem, (c, d))
            total += glz[c, src]
        gl_out[:, c * GL_LANES : (c + 1) * GL_LANES] = (total * scale_mine[:, :1]).astype(jnp.bfloat16)

    gw_acc[...] = jnp.zeros_like(gw_acc)

    def weight_step(step, carry):
        rt = right_t[pl.ds(pl.multiple_of(step * jb, jb), jb), :]
        for ac in range(0, chans, 2):
            at = slice(ac * rows, (ac + 2) * rows)
            oh[:, at], ol[:, at] = split(dot(rt, left[:, at], NN))
        for ac in range(0, chans, 8):
            total = gw_acc[ac * chans : (ac + 8) * chans, :]
            for jp in range(step_cols // 2):
                block = p_ref[pl.ds(step * step_cols + 2 * jp, 2)].reshape(2 * rows, width)
                for src in (oh, ol):
                    lhs = jnp.concatenate(
                        [
                            jnp.concatenate(
                                [
                                    src[j * chans : (j + 1) * chans, a * rows : (a + 1) * rows]
                                    for j in (2 * jp, 2 * jp + 1)
                                ],
                                axis=1,
                            )
                            for a in range(ac, ac + 8)
                        ],
                        axis=0,
                    )
                    total += dot(lhs, block, NN)
            gw_acc[ac * chans : (ac + 8) * chans, :] = total
        return carry

    lax.fori_loop(0, steps // 2, weight_step, 0)
    for c in range(chunks // 2):
        gl_second(c)
    lax.fori_loop(steps // 2, steps, weight_step, 0)

    half_rows, quarter, last = gw_r.shape[0], gw_y.shape[0], gw_z.shape[1]

    def span(start, size):
        return pl.ds(pl.multiple_of(start, 8), size)

    def gw_row():
        sent.append(send(gw_acc.at[span((1 - row) * half_rows, half_rows)], gw_r, gws_sem, (0,), {"row": 1 - row}))

    def gw_ypair():
        arrive(gw_r, gws_sem, (0,))
        gw_s1[...] = gw_acc[span(row * half_rows, half_rows), :] + gw_r[...]
        sent.append(send(gw_s1.at[span((1 - y) * quarter, quarter)], gw_y, gws_sem, (1,), {"seq": ypeer}))

    def gw_zs():
        arrive(gw_y, gws_sem, (1,))
        gw_s2[...] = gw_s1[span(y * quarter, quarter), :] + gw_y[...]
        for d in range(1, nz):
            sent.append(send(gw_s2.at[span(zs[d] * last, last)], gw_z.at[z], gwz_sem, (d,), {"seq": zs[d] * 2 + y}))

    def gw_place(r, yy, zz):
        return r * half_rows + yy * quarter + zz * last

    def gw_final():
        total = gw_s2[span(z * last, last), :]
        for d in range(1, nz):
            src = lax.rem(z + nz - d, nz)
            arrive(gw_z.at[src], gwz_sem, (d,))
            total += gw_z[src]
        mine = span(gw_place(row, y, z), last)
        gw_f[mine, :] = total / count
        for d in range(1, nz):
            sent.append(send(gw_f.at[mine], gw_f.at[mine], gwg_sem, (d,), {"seq": zs[d] * 2 + y}))

    def gw_gather_y():
        for d in range(1, nz):
            arrive(gw_f.at[span(gw_place(row, y, lax.rem(z + nz - d, nz)), last)], gwg_sem, (d,))
        mine = span(gw_place(row, y, 0), quarter)
        sent.append(send(gw_f.at[mine], gw_f.at[mine], gws_sem, (2,), {"seq": ypeer}))

    def gw_gather_row():
        arrive(gw_f.at[span(gw_place(row, 1 - y, 0), quarter)], gws_sem, (2,))
        mine = span(gw_place(row, 0, 0), half_rows)
        sent.append(send(gw_f.at[mine], gw_f.at[mine], gws_sem, (3,), {"row": 1 - row}))

    def gw_done():
        arrive(gw_f.at[span(gw_place(1 - row, 0, 0), half_rows)], gws_sem, (3,))
        gw_out[...] = gw_f[...]

    gw_row()
    for c in range(chunks // 2, chunks):
        gl_second(c)

    between = {0: gw_ypair, 1: gw_zs, 3: gw_final, 4: gw_gather_y}
    for step in range(max(steps, 6)):
        if step < steps:
            at = slice(step * jb, (step + 1) * jb)
            g = dot(qh[at, :], left[...], NT) + dot(ql[at, :], left[...], NT)
            gr_t[:, :, at] = g.T.reshape(shards, seq_rows, jb)
        if step in between:
            between[step]()

    collector = lax.div(me, nz) == row
    slot = lax.rem(me, nz)

    def row_copy():
        return pltpu.make_async_remote_copy(
            src_ref=gr_t, dst_ref=gr_r, send_sem=grr_sem.at[0], recv_sem=grr_sem.at[1],
            device_id={"row": 1 - row}, device_id_type=MESH,
        )

    def right_copy(o):
        e = lax.rem(me + o, shards)
        return pltpu.make_async_remote_copy(
            src_ref=gr_b.at[e], dst_ref=gr_in.at[slot], send_sem=gr_sem.at[0, o], recv_sem=gr_sem.at[1, slot],
            device_id={"seq": e}, device_id_type=MESH,
        )

    @pl.when(jnp.logical_not(collector))
    def _():
        row_copy().start()

    gw_gather_row()

    @pl.when(collector)
    def _():
        row_copy().wait_recv()
        scale3 = scale_all.reshape(shards, seq_rows, LANE)[:, :, :1]
        gr_b[...] = ((gr_t[...] + gr_r[...]) * scale3).astype(jnp.bfloat16)
        for o in range(1, shards):
            right_copy(o).start()
        gr_in[slot] = gr_b[me]

    for c in range(chunks):
        gl_last(c)
    gw_done()

    for k in range(nz):
        @pl.when(row * nz + k != me)
        def _():
            arrive(gr_in.at[k], gr_sem, (k,))

    gr_out[...] = gr_in[...]

    @pl.when(collector)
    def _():
        for o in range(1, shards):
            right_copy(o).wait_send()

    @pl.when(jnp.logical_not(collector))
    def _():
        row_copy().wait_send()

    for copy in sent:
        copy.wait_send()


def all_grads(pair_t, weight, left, right, chans):
    cols, rows, width = pair_t.shape
    shards, seq_rows, _ = right.shape
    nz = shards // 2
    seqs = shards * seq_rows
    lanes = chans * rows
    own = cols * chans
    jb = block_cols(cols) * chans
    chunks = lanes // GL_LANES
    total = chans * chans
    half, quarter, last = total // 2, total // 4, total // 4 // nz
    f32, bf16 = jnp.float32, jnp.bfloat16
    flops = 2 * cols * rows * chans * chans * (width * 3 + seqs * 5)
    vmem = pl.BlockSpec(memory_space=pltpu.VMEM)
    sem = pltpu.SemaphoreType.DMA
    return pl.pallas_call(
        functools.partial(kernel, shards, chans),
        in_specs=[vmem] * 4,
        out_specs=[vmem] * 3,
        out_shape=[
            jax.ShapeDtypeStruct((seq_rows, lanes), bf16),
            jax.ShapeDtypeStruct((nz, seq_rows, own), bf16),
            jax.ShapeDtypeStruct((total, width), f32),
        ],
        scratch_shapes=[
            pltpu.VMEM((own, lanes), bf16),
            pltpu.VMEM((own, lanes), bf16),
            pltpu.VMEM((jb, lanes), bf16),
            pltpu.VMEM((jb, lanes), bf16),
            pltpu.VMEM((shards, seq_rows, lanes), bf16),
            pltpu.VMEM((shards, seq_rows, LANE + own), bf16),
            pltpu.VMEM((seqs, lanes), bf16),
            pltpu.VMEM((seqs, own), bf16),
            pltpu.VMEM((own, seqs), bf16),
            pltpu.VMEM((chunks, 2, nz, seq_rows, GL_LANES), f32),
            pltpu.VMEM((chunks, nz, seq_rows, GL_LANES), f32),
            pltpu.VMEM((chunks, nz, seq_rows, GL_LANES), f32),
            pltpu.VMEM((chunks, nz, seq_rows, GL_LANES), f32),
            pltpu.VMEM((shards, seq_rows, own), f32),
            pltpu.VMEM((shards, seq_rows, own), f32),
            pltpu.VMEM((shards, seq_rows, own), bf16),
            pltpu.VMEM((nz, seq_rows, own), bf16),
            pltpu.VMEM((total, width), f32),
            pltpu.VMEM((half, width), f32),
            pltpu.VMEM((half, width), f32),
            pltpu.VMEM((quarter, width), f32),
            pltpu.VMEM((quarter, width), f32),
            pltpu.VMEM((nz, last, width), f32),
            pltpu.VMEM((total, width), f32),
            sem((2, shards)),
            sem((2, nz)),
            sem((2, nz)),
            sem((2, chunks)),
            sem((2, chunks, nz)),
            sem((2,)),
            sem((2, shards)),
            sem((2, 4)),
            sem((2, nz)),
            sem((2, nz)),
        ],
        compiler_params=pltpu.CompilerParams(
            vmem_limit_bytes=56 * 2**20, collective_id=0, has_side_effects=True
        ),
        cost_estimate=pl.CostEstimate(flops=flops, bytes_accessed=6 * 2**20, transcendentals=0),
        name="all_grads",
    )(pair_t, weight, left, right)


def body(left_act, right_act, pair_grad, out_weight, seq_mask):
    seq_rows, pair_rows, chans = left_act.shape
    shards = lax.axis_size("seq")
    cols = right_act.shape[1]
    mask_half = seq_mask.astype(jnp.bfloat16)[:, None, None]
    left = (left_act * mask_half).transpose(0, 2, 1).reshape(seq_rows, chans * pair_rows)
    right = (right_act * mask_half).reshape(seq_rows, shards, -1)
    marks = jnp.broadcast_to(mask_half, (seq_rows, shards, LANE))
    right = jnp.concatenate([marks, right], axis=2).transpose(1, 0, 2)
    gl, gr, gw = all_grads(pair_grad.transpose(1, 0, 2), out_weight, left, right, chans)
    grad_left = gl.reshape(seq_rows, chans, pair_rows).transpose(0, 2, 1)
    grad_right = gr.transpose(1, 0, 2).reshape(seq_rows, -1, chans)
    return (grad_left, grad_right, gw)


def solution(mesh):
    placed = (
        P(("grp", "seq"), "row", None),
        P(("grp", "seq"), None, None),
        P(("grp", "row"), "seq", None),
        P(),
        P(("grp", "seq")),
    )
    return jax.shard_map(
        body,
        mesh=mesh,
        in_specs=placed,
        out_specs=(P(("grp", "seq"), "row", None), P(("grp", "seq"), "row", None), P("grp", None)),
        check_vma=False,
    )
```

```python
import functools

import jax
import jax.numpy as jnp
from jax import lax
from jax.experimental import pallas as pl
from jax.experimental.pallas import tpu as pltpu
from jax.sharding import PartitionSpec as P

NT = (((1,), (1,)), ((), ()))
NN = (((1,), (0,)), ((), ()))
MESH = pl.DeviceIdType.MESH
GL_LANES = 1024
LANE = 128
PROJECT = 4
HALVES = 2


def block_cols(cols):
    return max(n for n in (2, 4, 6, 8) if cols % n == 0)


def dot(lhs, rhs, dims):
    return lax.dot_general(lhs, rhs, dims, preferred_element_type=jnp.float32)


def split(value):
    high = value.astype(jnp.bfloat16)
    low = (value - high.astype(jnp.float32)).astype(jnp.bfloat16)
    return high, low


def kernel(
    shards, chans, p_ref, w_ref, l_in, r_in, gl_out, gr_out, gw_out,
    qh, ql, oh, ol, l_all, r_all, left, right, right_t,
    part, gly, gls, glz, gr_t, gr_r, gr_b, gr_in,
    gw_acc, gw_r, gw_s1, gw_y, gw_s2, gw_z, gw_f,
    r_sem, lz_sem, ly_sem, gly_sem, glz_sem, grr_sem, gr_sem, gws_sem, gwz_sem, gwg_sem,
):
    cols, rows, width = p_ref.shape
    nz = shards // 2
    chunks = part.shape[0]
    seq_rows = l_in.shape[0]
    seqs = shards * seq_rows
    step_cols = block_cols(cols)
    steps = cols // step_cols
    jb = step_cols * chans
    own_cols = cols * chans
    me = lax.axis_index("seq")
    row = lax.axis_index("row")
    y, z = lax.rem(me, 2), lax.div(me, 2)
    ypeer, zs = z * 2 + 1 - y, [lax.rem(z + d, nz) for d in range(nz)]
    sent = []

    def send(src, dst, sems, at, where, recv_at=None):
        copy = pltpu.make_async_remote_copy(
            src_ref=src, dst_ref=dst, send_sem=sems.at[(0,) + at],
            recv_sem=sems.at[(1,) + (at if recv_at is None else recv_at)],
            device_id=where, device_id_type=MESH,
        )
        copy.start()
        return copy

    def arrive(dst, sems, at):
        pltpu.make_async_remote_copy(
            src_ref=dst, dst_ref=dst, send_sem=sems.at[(0,) + at], recv_sem=sems.at[(1,) + at],
            device_id={"seq": ypeer}, device_id_type=MESH,
        ).wait_recv()

    barrier = pltpu.get_barrier_semaphore()
    for o in range(1, shards):
        pl.semaphore_signal(barrier, inc=1, device_id={"seq": lax.rem(me + o, shards)}, device_id_type=MESH)
    pl.semaphore_signal(barrier, inc=1, device_id={"row": 1 - row}, device_id_type=MESH)
    pl.semaphore_wait(barrier, shards)

    for o in range(1, shards):
        e = lax.rem(me + o, shards)
        sent.append(send(r_in.at[e], r_all.at[me], r_sem, (o,), {"seq": e}))
    l_all[me] = l_in[...]
    r_all[me] = r_in[me]

    def project(jp, carry):
        block = p_ref[pl.ds(jp * 2, 2)].reshape(2 * rows, width)
        for ac in range(0, chans, PROJECT):
            q = dot(w_ref[ac * chans : (ac + PROJECT) * chans, :], block, NT)
            high, low = split(q)
            for a in range(PROJECT):
                for jj in range(2):
                    base = pl.multiple_of((jp * 2 + jj) * chans, chans)
                    to = (pl.ds(base, chans), slice((ac + a) * rows, (ac + a + 1) * rows))
                    at = (slice(a * chans, (a + 1) * chans), slice(jj * rows, (jj + 1) * rows))
                    qh[to] = high[at]
                    ql[to] = low[at]
        return carry

    pairs = cols // 2
    first = pairs // 6
    lax.fori_loop(0, first, project, 0)
    for d in range(1, nz):
        sent.append(send(l_in, l_all.at[me], lz_sem, (d,), {"seq": zs[d] * 2 + y}))
    sent.append(send(l_in, l_all.at[me], ly_sem, (0,), {"seq": ypeer}))
    lax.fori_loop(first, pairs, project, 0)

    for o in range(1, shards):
        arrive(r_all.at[lax.rem(me + shards - o, shards)], r_sem, (o,))
    rfull = r_all[...].astype(jnp.float32).reshape(seqs, LANE + own_cols)
    mask_all = rfull[:, :LANE]
    count = jnp.sum(mask_all, axis=0, keepdims=True)
    scale_all = mask_all / count
    scale_mine = r_in[me].astype(jnp.float32)[:, :LANE] / count
    right[...] = rfull[:, LANE:].astype(jnp.bfloat16)
    right_t[...] = rfull[:, LANE:].T.astype(jnp.bfloat16)

    def gl_first(c):
        for t in range(0, GL_LANES, 256):
            at = slice(c * GL_LANES + t, c * GL_LANES + t + 256)
            g = dot(right[...], qh[:, at], NN) + dot(right[...], ql[:, at], NN)
            g = g.reshape(nz, 2, seq_rows, 256)
            for half in range(2):
                part[c, half, :, :, t : t + 256] = g[:, half]
        sent.append(send(part.at[c, 1 - y], gly.at[c], gly_sem, (c,), {"seq": ypeer}))

    early = chunks
    gl_first(0)
    for d in range(1, nz):
        src = lax.rem(z + nz - d, nz) * 2 + y
        arrive(l_all.at[src], lz_sem, (d,))
        sent.append(send(l_all.at[src], l_all.at[src], ly_sem, (d,), {"seq": ypeer}))
    for c in range(1, early):
        gl_first(c)

    for d in range(nz):
        src = lax.rem(z + nz - d, nz) * 2 + 1 - y
        arrive(l_all.at[src], ly_sem, (d,))
    left[...] = l_all[...].astype(jnp.float32).reshape(seqs, -1).astype(jnp.bfloat16)

    def gl_second(c):
        arrive(gly.at[c], gly_sem, (c,))
        gls[c] = part[c, y] + gly[c]
        for d in range(1, nz):
            sent.append(send(gls.at[c, zs[d]], glz.at[c, z], glz_sem, (c, d), {"seq": zs[d] * 2 + y}))

    def gl_last(c):
        total = gls[c, z]
        for d in range(1, nz):
            src = lax.rem(z + nz - d, nz)
            arrive(glz.at[c, src], glz_sem, (c, d))
            total += glz[c, src]
        gl_out[:, c * GL_LANES : (c + 1) * GL_LANES] = (total * scale_mine[:, :1]).astype(jnp.bfloat16)

    gw_acc[...] = jnp.zeros_like(gw_acc)
    piece_chans = chans // gw_r.shape[0]

    def weight_step(piece, step):
        rt = right_t[pl.ds(pl.multiple_of(step * jb, jb), jb), :]
        begin, end = piece * piece_chans, (piece + 1) * piece_chans
        for ac in range(begin, end, 2):
            at = slice(ac * rows, (ac + 2) * rows)
            to = slice((ac - begin) * rows, (ac - begin + 2) * rows)
            oh[:, to], ol[:, to] = split(dot(rt, left[:, at], NN))
        for ac in range(0, piece_chans, 8):
            out = slice((begin + ac) * chans, (begin + ac + 8) * chans)
            total = gw_acc[out, :]
            for jp in range(step_cols // 2):
                block = p_ref[pl.ds(step * step_cols + 2 * jp, 2)].reshape(2 * rows, width)
                for src in (oh, ol):
                    lhs = jnp.concatenate(
                        [
                            jnp.concatenate(
                                [
                                    src[j * chans : (j + 1) * chans, a * rows : (a + 1) * rows]
                                    for j in (2 * jp, 2 * jp + 1)
                                ],
                                axis=1,
                            )
                            for a in range(ac, ac + 8)
                        ],
                        axis=0,
                    )
                    total += dot(lhs, block, NN)
            gw_acc[out, :] = total

    def weight_steps(piece, start, stop):
        def one(step, carry):
            weight_step(piece, step)
            return carry

        lax.fori_loop(start, stop, one, 0)

    piece_rows = piece_chans * chans
    half_rows, quarter, last = gw_r.shape[1], gw_y.shape[1], gw_z.shape[2]

    def span(start, size):
        return pl.ds(pl.multiple_of(start, 8), size)

    def gw_place(h, r, yy, zz):
        return h * piece_rows + r * half_rows + yy * quarter + zz * last

    def gw_row(h):
        src = gw_acc.at[span(gw_place(h, 1 - row, 0, 0), half_rows)]
        sent.append(send(src, gw_r.at[h], gws_sem, (h, 0), {"row": 1 - row}))

    def gw_ypair(h):
        arrive(gw_r.at[h], gws_sem, (h, 0))
        gw_s1[h] = gw_acc[span(gw_place(h, row, 0, 0), half_rows), :] + gw_r[h]
        sent.append(send(gw_s1.at[h, span((1 - y) * quarter, quarter)], gw_y.at[h], gws_sem, (h, 1), {"seq": ypeer}))

    def gw_zs(h):
        arrive(gw_y.at[h], gws_sem, (h, 1))
        gw_s2[h] = gw_s1[h, span(y * quarter, quarter), :] + gw_y[h]
        for d in range(1, nz):
            src = gw_s2.at[h, span(zs[d] * last, last)]
            sent.append(send(src, gw_z.at[h, z], gwz_sem, (h, d), {"seq": zs[d] * 2 + y}))

    def gw_final(h):
        total = gw_s2[h, span(z * last, last), :]
        for d in range(1, nz):
            src = lax.rem(z + nz - d, nz)
            arrive(gw_z.at[h, src], gwz_sem, (h, d))
            total += gw_z[h, src]
        mine = span(gw_place(h, row, y, z), last)
        gw_f[mine, :] = total / count
        for d in range(1, nz):
            sent.append(send(gw_f.at[mine], gw_f.at[mine], gwg_sem, (h, d), {"seq": zs[d] * 2 + y}))

    def gw_gather_y(h):
        for d in range(1, nz):
            src = lax.rem(z + nz - d, nz)
            arrive(gw_f.at[span(gw_place(h, row, y, src), last)], gwg_sem, (h, d))
        mine = span(gw_place(h, row, y, 0), quarter)
        sent.append(send(gw_f.at[mine], gw_f.at[mine], gws_sem, (h, 2), {"seq": ypeer}))

    def gw_gather_row(h):
        arrive(gw_f.at[span(gw_place(h, row, 1 - y, 0), quarter)], gws_sem, (h, 2))
        mine = span(gw_place(h, row, 0, 0), half_rows)
        sent.append(send(gw_f.at[mine], gw_f.at[mine], gws_sem, (h, 3), {"row": 1 - row}))

    def gw_done(h):
        arrive(gw_f.at[span(gw_place(h, 1 - row, 0, 0), half_rows)], gws_sem, (h, 3))

    pieces = range(gw_r.shape[0])
    last_piece = len(pieces) - 1
    middle = steps // 2
    weight_steps(0, 0, middle)
    for c in range(chunks // 2):
        gl_second(c)
    weight_steps(0, middle, steps)
    gw_row(0)
    if last_piece:
        weight_steps(1, 0, middle)
    gw_ypair(0)
    for c in range(chunks // 2, chunks):
        gl_second(c)
    if last_piece:
        weight_steps(1, middle, steps)
        gw_row(1)
    gw_zs(0)

    between = {2: [lambda: gw_final(0)]}
    if last_piece:
        between[0] = [lambda: gw_ypair(1)]
        between[4] = [lambda: gw_zs(1)]
    for step in range(max(steps, 6)):
        if step < steps:
            at = slice(step * jb, (step + 1) * jb)
            g = dot(qh[at, :], left[...], NT) + dot(ql[at, :], left[...], NT)
            gr_t[:, :, at] = g.T.reshape(shards, seq_rows, jb)
        for act in between.get(step, []):
            act()

    collector = lax.div(me, nz) == row
    slot = lax.rem(me, nz)

    def row_copy():
        return pltpu.make_async_remote_copy(
            src_ref=gr_t, dst_ref=gr_r, send_sem=grr_sem.at[0], recv_sem=grr_sem.at[1],
            device_id={"row": 1 - row}, device_id_type=MESH,
        )

    def right_copy(o):
        e = lax.rem(me + o, shards)
        return pltpu.make_async_remote_copy(
            src_ref=gr_b.at[e], dst_ref=gr_in.at[slot], send_sem=gr_sem.at[0, o], recv_sem=gr_sem.at[1, slot],
            device_id={"seq": e}, device_id_type=MESH,
        )

    @pl.when(jnp.logical_not(collector))
    def _():
        row_copy().start()

    gw_gather_y(0)
    if last_piece:
        gw_final(1)

    @pl.when(collector)
    def _():
        row_copy().wait_recv()
        scale3 = scale_all.reshape(shards, seq_rows, LANE)[:, :, :1]
        gr_b[...] = ((gr_t[...] + gr_r[...]) * scale3).astype(jnp.bfloat16)
        for o in range(1, shards):
            right_copy(o).start()
        gr_in[slot] = gr_b[me]

    gw_gather_row(0)
    if last_piece:
        gw_gather_y(1)
    for c in range(chunks):
        gl_last(c)
    if last_piece:
        gw_gather_row(1)
    for h in pieces:
        gw_done(h)
    gw_out[...] = gw_f[...]

    for k in range(nz):
        @pl.when(row * nz + k != me)
        def _():
            arrive(gr_in.at[k], gr_sem, (k,))

    gr_out[...] = gr_in[...]

    @pl.when(collector)
    def _():
        for o in range(1, shards):
            right_copy(o).wait_send()

    @pl.when(jnp.logical_not(collector))
    def _():
        row_copy().wait_send()

    for copy in sent:
        copy.wait_send()


def all_grads(pair_t, weight, left, right, chans):
    cols, rows, width = pair_t.shape
    shards, seq_rows, _ = right.shape
    nz = shards // 2
    seqs = shards * seq_rows
    lanes = chans * rows
    own = cols * chans
    jb = block_cols(cols) * chans
    chunks = lanes // GL_LANES
    total = chans * chans
    pieces = HALVES if total // HALVES // 4 // nz >= 8 else 1
    half, quarter, last = total // pieces // 2, total // pieces // 4, total // pieces // 4 // nz
    f32, bf16 = jnp.float32, jnp.bfloat16
    flops = 2 * cols * rows * chans * chans * (width * 3 + seqs * 5)
    vmem = pl.BlockSpec(memory_space=pltpu.VMEM)
    sem = pltpu.SemaphoreType.DMA
    return pl.pallas_call(
        functools.partial(kernel, shards, chans),
        in_specs=[vmem] * 4,
        out_specs=[vmem] * 3,
        out_shape=[
            jax.ShapeDtypeStruct((seq_rows, lanes), bf16),
            jax.ShapeDtypeStruct((nz, seq_rows, own), bf16),
            jax.ShapeDtypeStruct((total, width), f32),
        ],
        scratch_shapes=[
            pltpu.VMEM((own, lanes), bf16),
            pltpu.VMEM((own, lanes), bf16),
            pltpu.VMEM((jb, lanes // pieces), bf16),
            pltpu.VMEM((jb, lanes // pieces), bf16),
            pltpu.VMEM((shards, seq_rows, lanes), bf16),
            pltpu.VMEM((shards, seq_rows, LANE + own), bf16),
            pltpu.VMEM((seqs, lanes), bf16),
            pltpu.VMEM((seqs, own), bf16),
            pltpu.VMEM((own, seqs), bf16),
            pltpu.VMEM((chunks, 2, nz, seq_rows, GL_LANES), f32),
            pltpu.VMEM((chunks, nz, seq_rows, GL_LANES), f32),
            pltpu.VMEM((chunks, nz, seq_rows, GL_LANES), f32),
            pltpu.VMEM((chunks, nz, seq_rows, GL_LANES), f32),
            pltpu.VMEM((shards, seq_rows, own), f32),
            pltpu.VMEM((shards, seq_rows, own), f32),
            pltpu.VMEM((shards, seq_rows, own), bf16),
            pltpu.VMEM((nz, seq_rows, own), bf16),
            pltpu.VMEM((total, width), f32),
            pltpu.VMEM((pieces, half, width), f32),
            pltpu.VMEM((pieces, half, width), f32),
            pltpu.VMEM((pieces, quarter, width), f32),
            pltpu.VMEM((pieces, quarter, width), f32),
            pltpu.VMEM((pieces, nz, last, width), f32),
            pltpu.VMEM((total, width), f32),
            sem((2, shards)),
            sem((2, nz)),
            sem((2, nz)),
            sem((2, chunks)),
            sem((2, chunks, nz)),
            sem((2,)),
            sem((2, shards)),
            sem((2, pieces, 4)),
            sem((2, pieces, nz)),
            sem((2, pieces, nz)),
        ],
        compiler_params=pltpu.CompilerParams(
            vmem_limit_bytes=56 * 2**20, collective_id=0, has_side_effects=True
        ),
        cost_estimate=pl.CostEstimate(flops=flops, bytes_accessed=6 * 2**20, transcendentals=0),
        name="all_grads",
    )(pair_t, weight, left, right)


def body(left_act, right_act, pair_grad, out_weight, seq_mask):
    seq_rows, pair_rows, chans = left_act.shape
    shards = lax.axis_size("seq")
    cols = right_act.shape[1]
    mask_half = seq_mask.astype(jnp.bfloat16)[:, None, None]
    left = (left_act * mask_half).transpose(0, 2, 1).reshape(seq_rows, chans * pair_rows)
    right = (right_act * mask_half).reshape(seq_rows, shards, -1)
    marks = jnp.broadcast_to(mask_half, (seq_rows, shards, LANE))
    right = jnp.concatenate([marks, right], axis=2).transpose(1, 0, 2)
    gl, gr, gw = all_grads(pair_grad.transpose(1, 0, 2), out_weight, left, right, chans)
    grad_left = gl.reshape(seq_rows, chans, pair_rows).transpose(0, 2, 1)
    grad_right = gr.transpose(1, 0, 2).reshape(seq_rows, -1, chans)
    return (grad_left, grad_right, gw)


def solution(mesh):
    placed = (
        P(("grp", "seq"), "row", None),
        P(("grp", "seq"), None, None),
        P(("grp", "row"), "seq", None),
        P(),
        P(("grp", "seq")),
    )
    return jax.shard_map(
        body,
        mesh=mesh,
        in_specs=placed,
        out_specs=(P(("grp", "seq"), "row", None), P(("grp", "seq"), "row", None), P("grp", None)),
        check_vma=False,
    )
```
